128 devices in a mesh: dp: 8 (over z, core), tensor: 16 (over x, y).
Axes of the slice: x: 4, y: 4, z: 4, core: 2. Of those that a mesh axis runs over, the one named last changes fastest.
Arguments:
- queries: bfloat16 [512, 6144], P('dp', 'tensor'), may hold values from -4.5 to 4.5
- key_cache: bfloat16 [512, 16, 128, 128], P('dp', 'tensor'), may hold values from -4.5 to 4.5
- value_cache: bfloat16 [512, 16, 128, 128], P('dp', 'tensor'), may hold values from -6 to 6
- lengths: int32 [512], P('dp'), may hold values from 2 to 128, as said below
- out_proj: bfloat16 [6144, 6144], P('tensor'), may hold values from -0.75 to 0.75
- residual: bfloat16 [512, 6144], P('dp'), may hold values from -6 to 6
- norm_gain: bfloat16 [6144], replicated, may hold values from 0.099609375 to 1.8984375
- expert_ids: int32 [512, 2], P('dp'), may hold values from 0 to 7, all different within a row; in each aligned block of 64 rows (0 to 63, 64 to 127, ...) at most 24 rows name the same one
- gate_weights: float32 [512, 2], P('dp'), may hold values from 0.2 to 1
- w_gate: bfloat16 [8, 6144, 8192], P('dp', None, 'tensor'), may hold values from -0.078125 to 0.078125
- w_up: bfloat16 [8, 6144, 8192], P('dp', None, 'tensor'), may hold values from -0.078125 to 0.078125
- w_down: bfloat16 [8, 8192, 6144], P('dp', 'tensor'), may hold values from -0.09375 to 0.09375
Outputs:
- layer_out: bfloat16 [512, 6144], P('dp', 'tensor')
The draws below stay inside these ranges and needn't reach their ends.
Inputs may be any that keep to these rules, and one draw needn't show every extreme that they name: Row r uses cache positions 0 to lengths[r] - 1; in every aligned block of 64 rows some row has exactly 128. `expert_ids`: each row names two different experts; within each aligned block of 64 rows no expert is named by more than 24 rows, a bound that some block reaches.
All inputs are finite; a program needn't handle non-finite values.
Results may differ from the reference program's by a relative error of at most 0.0059.
Values may be sent and summed in bfloat16 or wider, within the bound.
A program may use at most 128 MiB of HBM per device.

```python
import math
import jax
import jax.numpy as jnp
import numpy as np
from jax import lax

D = 6144
H = 48
KVH = 8
HD = 128
FF = 8192
ROWS_DEV = 64
CACHE = 128
ROWS = 512
EXPERTS = 8
SLOTS = 16
CAP = 24
N_DP = 8


def draw_queries(key, part):
    key = jax.random.fold_in(key, 11)
    values = jnp.clip(jax.random.normal(key, (ROWS, H, HD), jnp.float32), -4.5, 4.5)
    return values.reshape(ROWS, H * HD).astype(jnp.bfloat16)


def draw_key_cache(key, part):
    key = jax.random.fold_in(key, 12)
    base_keys = jnp.clip(jax.random.normal(key, (ROWS, KVH, CACHE, HD), jnp.float32), -4.5, 4.5)
    slot_heads = jnp.arange(SLOTS) * KVH // SLOTS
    return base_keys[:, slot_heads].astype(jnp.bfloat16)


def draw_lengths(key, part):
    key = jax.random.fold_in(key, 13)
    drawn = jax.random.randint(key, (ROWS,), 2, CACHE + 1)
    chosen = jax.random.randint(jax.random.fold_in(key, 1), (ROWS // ROWS_DEV,), 0, ROWS_DEV)
    row_index = jnp.arange(ROWS)
    longest = row_index % ROWS_DEV == chosen[row_index // ROWS_DEV]
    return jnp.where(longest, CACHE, drawn).astype(jnp.int32)


def strengthened(entries, key, source, target, parts, factor):
    def block_of(dim):
        return (jnp.arange(entries.shape[dim]) // (entries.shape[dim] // parts)).reshape((-1,) + (1,) * (entries.ndim - 1 - dim))

    first = jax.random.permutation(key, parts)[block_of(target)]
    second = (block_of(target) + parts // 2) % parts
    return jnp.where((block_of(source) == first) | (block_of(source) == second), factor * entries, entries)


def steps_of(stream_key, extent, shards, least, high):
    level = 1.0
    for dim, shards_of in shards:
        steps = jax.random.uniform(jax.random.fold_in(jax.random.fold_in(stream_key, 6), dim), (shards_of,), jnp.float32, least / len(shards), high / len(shards))
        level = level * jnp.repeat(jnp.exp(steps), extent[dim] // shards_of).reshape((-1,) + (1,) * (len(extent) - 1 - dim))
    return level


def deal_out(own_key, own, number, rows, amount, top, reach, skew):
    sequence = jax.random.permutation(own_key, amount)
    heavy_load, ordinary = shares(amount, rows * top, reach, skew, True), shares(amount, rows * top, reach, skew, False)
    places = jnp.arange(amount)

    def named(tallies, offset_by):
        used = int((tallies > 0).sum())
        fixed = max(1, used // 4)
        moved = fixed + (places - fixed + offset_by * (used - fixed)) % max(1, amount - fixed)
        return jnp.zeros((amount,), jnp.int32).at[sequence[jnp.where(places < fixed, places, moved)]].set(jnp.asarray(tallies, jnp.int32))

    tallies = jnp.where(number % 4 == 0, named(heavy_load, number // 4), named(ordinary, number - number // 4 - 1))
    mixed = jax.random.permutation(jax.random.fold_in(own, 3), amount)
    donor, receiver = mixed[0:amount // 2 * 2:2], mixed[1:amount // 2 * 2:2]
    slack = jnp.minimum(tallies[donor] - 1, reach - tallies[receiver]) // 2
    slack = jnp.where((donor == sequence[0]) | (receiver == sequence[0]) | (tallies[receiver] == 0), 0, jnp.maximum(slack, 0))
    moved = jax.random.randint(jax.random.fold_in(own, 4), (amount // 2,), 0, 1 << 20) % (slack + 1)
    tallies = tallies.at[donor].add(-moved).at[receiver].add(moved)
    members = jnp.searchsorted(jnp.cumsum(tallies), jnp.arange(rows * top), side="right").astype(jnp.int32)
    table = members.reshape(top, rows).T
    table = table[jax.random.permutation(jax.random.fold_in(own, 1), rows)]
    offset_by = jax.random.randint(jax.random.fold_in(own, 2), (rows, 1), 0, top)
    return jnp.take_along_axis(table, (jnp.arange(top)[None, :] + offset_by) % top, axis=1)


def shares(count, total, most, skew, full):
    portions = [(1 << 20) // math.isqrt(standing ** skew) + 1 for standing in range(1, count + 1)]
    largest = most if full else min(most, max(-(-total // count), total * portions[0] // sum(portions)))
    least = 1 if total - largest >= count - 1 else 0
    holding, surplus = [largest] + [least] * (count - 1), total - largest - least * (count - 1)
    while surplus > 0:
        movable = [i for i in range(1, count) if holding[i] < largest] or [i for i in range(1, count) if holding[i] < most]
        mass, budget = sum([portions[i] for i in movable]), surplus
        for i in movable:
            addition = min(most - holding[i], max(1, budget * portions[i] // mass), surplus)
            holding[i] = holding[i] + addition
            surplus = surplus - addition
    return np.array(holding)


def centred(stream_key, extent, deviation, most, split=(), kind=jnp.bfloat16):
    level = steps_of(stream_key, extent, split, -0.22, 0.18) if split else 1.0
    values = jax.random.normal(stream_key, extent, jnp.float32) * deviation * level
    return jnp.minimum(jnp.maximum(values, -most), most).astype(kind)


def noise_with(own_key, dims, spread, limit, split, heavy, kind=jnp.bfloat16):
    array = spread * jax.random.normal(own_key, dims, jnp.float32)
    if split:
        array = array * steps_of(own_key, dims, split, -0.22, 0.18)
    return jnp.clip(strengthened(array, jax.random.fold_in(own_key, 3), *heavy), -limit, limit).astype(kind)


def setup_inputs(seed: int = 0) -> dict:
    splits = jax.random.split(jax.random.key(seed), 13)
    queries = draw_queries(jax.random.fold_in(splits[12], 71), 0)
    key_cache = draw_key_cache(jax.random.fold_in(splits[12], 71), 0)
    value_cache = centred(splits[2], (ROWS, SLOTS, CACHE, HD), 1.0, 6.0, ((0, 8), (1, 16)))
    lengths = draw_lengths(jax.random.fold_in(splits[12], 71), 0)
    out_proj = noise_with(splits[4], (H * HD, D), HD ** -0.5, 0.75, ((0, 16),), (0, 1, 16, 2.0))
    residual = centred(splits[5], (ROWS, D), 1.0, 6.0, ((0, 8),))
    norm_gain = jnp.clip(1.0 + 0.18 * jax.random.normal(splits[6], (D,), jnp.float32), 0.099609375, 1.8984375).astype(jnp.bfloat16)
    expert_ids_keys = jax.random.split(jax.random.fold_in(splits[7], 1), ROWS // ROWS_DEV)
    expert_ids_turns = jax.random.permutation(jax.random.fold_in(splits[7], 3), ROWS // ROWS_DEV)
    expert_ids = jax.vmap(lambda own, number: deal_out(jax.random.fold_in(splits[7], 2), own, number, ROWS_DEV, EXPERTS, 2, CAP, 2))(expert_ids_keys, expert_ids_turns).reshape((ROWS, 2))
    gate_weights = jnp.clip(0.2 + 0.8 * jax.random.uniform(splits[8], (ROWS, 2), jnp.float32) ** steps_of(splits[8], (ROWS, 2), ((0, 8),), -0.2, 0.2), 0.2, 1.0)
    w_gate = centred(splits[9], (EXPERTS, D, FF), D ** -0.5, 0.078125, ((0, 8), (2, 16)))
    w_up = centred(splits[10], (EXPERTS, D, FF), D ** -0.5, 0.078125, ((0, 8), (2, 16)))
    w_down = noise_with(splits[11], (EXPERTS, FF, D), FF ** -0.5, 0.09375, ((0, 8), (1, 16)), (1, 2, 16, 2.0))
    return {"queries": queries, "key_cache": key_cache, "value_cache": value_cache, "lengths": lengths, "out_proj": out_proj, "residual": residual, "norm_gain": norm_gain, "expert_ids": expert_ids, "gate_weights": gate_weights, "w_gate": w_gate, "w_up": w_up, "w_down": w_down}


def reference(queries, key_cache, value_cache, lengths, out_proj, residual, norm_gain, expert_ids, gate_weights, w_gate, w_up, w_down):
    group_size = H // SLOTS
    query_grid = queries.astype(jnp.float32).reshape(ROWS, SLOTS, group_size, HD)
    scores = jnp.einsum('rsgd,rscd->rsgc', query_grid, key_cache.astype(jnp.float32)) * HD ** (-0.5)
    visible = jnp.arange(CACHE)[None, :] < lengths[:, None]
    scores = jnp.where(visible[:, None, None, :], scores, -1e+30)
    row_max = lax.optimization_barrier(jnp.max(scores, axis=-1, keepdims=True))
    exp_scores = jnp.exp(scores - row_max)
    weights = (exp_scores / lax.optimization_barrier(jnp.sum(exp_scores, axis=-1, keepdims=True))).astype(jnp.bfloat16)
    combined = jnp.einsum('rsgc,rscd->rsgd', weights.astype(jnp.float32), value_cache.astype(jnp.float32))
    attended = combined.astype(jnp.bfloat16).reshape(ROWS, H * HD)
    hidden = residual.astype(jnp.float32) + jnp.dot(attended, out_proj, preferred_element_type=jnp.float32)
    inverse = lax.rsqrt(lax.optimization_barrier(jnp.mean(hidden * hidden, axis=1, keepdims=True)) + 1e-05)
    normed = (hidden * inverse * norm_gain.astype(jnp.float32)).astype(jnp.bfloat16)
    slot_limit = N_DP * CAP

    def one_expert(expert, running):
        is_named = expert_ids == expert
        weight = lax.optimization_barrier(jnp.sum(jnp.where(is_named, gate_weights, 0.0), axis=1))
        flags = jnp.where(jnp.any(is_named, axis=1), 0, 1).astype(jnp.int32)
        row_order = jnp.argsort(flags, stable=True)[:slot_limit].astype(jnp.int32)
        picked = normed[row_order]
        gate_mat = lax.dynamic_index_in_dim(w_gate, expert, 0, keepdims=False)
        up_mat = lax.dynamic_index_in_dim(w_up, expert, 0, keepdims=False)
        down_mat = lax.dynamic_index_in_dim(w_down, expert, 0, keepdims=False)
        gate_value = jnp.dot(picked, gate_mat, preferred_element_type=jnp.float32)
        up_value = jnp.dot(picked, up_mat, preferred_element_type=jnp.float32)
        active = (jax.nn.silu(gate_value) * up_value).astype(jnp.bfloat16)
        result = jnp.dot(active, down_mat, preferred_element_type=jnp.float32).astype(jnp.bfloat16)
        return running.at[row_order].add(weight[row_order][:, None] * result.astype(jnp.float32))
    experts_sum = lax.fori_loop(0, EXPERTS, one_expert, jnp.zeros((ROWS, D), jnp.float32))
    return (hidden + experts_sum).astype(jnp.bfloat16)
```

```python
import math

import jax
import jax.numpy as jnp
from jax import lax
from jax.experimental import pallas as pl
from jax.experimental.pallas import tpu as pltpu
from jax.sharding import PartitionSpec as P

HD = 128
CAP = 24
PAD = 32
EPSILON = 1e-05
F32 = jnp.float32
BF16 = jnp.bfloat16
N_SEMS = 8 + 28 + 36 + 1 + 1

ORDER = (
    (2, 2), (1, 2), (3, 2), (2, 1), (2, 3), (1, 1), (1, 3), (3, 1), (3, 3),
    (2, 0), (0, 2), (1, 0), (3, 0), (0, 1), (0, 3), (0, 0),
)


class Links:
    def __init__(self, send_sem, recv_sem, to):
        self.send_sem, self.recv_sem, self.to = send_sem, recv_sem, to
        self.sent = 0
        self.numbers = {}

    def copy(self, key, src, dst, where):
        number = self.numbers.setdefault(key, len(self.numbers))
        return pltpu.make_async_remote_copy(
            src_ref=src,
            dst_ref=dst,
            send_sem=self.send_sem.at[0],
            recv_sem=self.recv_sem.at[number],
            device_id=self.to[where],
            device_id_type=pl.DeviceIdType.MESH,
        )

    def send(self, key, src, dst, where):
        self.copy(key, src, dst, where).start()
        self.sent += math.prod(src.shape)

    def arrived(self, key, dst):
        self.copy(key, dst, dst, "x+").wait_recv()

    def finish(self, space):
        space = space.at[pl.ds(0, self.sent // space.shape[1])]
        self.copy(next(iter(self.numbers)), space, space, "x+").wait_send()


def f32(value):
    return value.astype(F32)


class Quarter:
    def __init__(self, links, index, rows, axes, side):
        self.links, self.index, self.axes, self.side = links, index, axes, side
        self.rows = pl.ds(index * rows, rows)

    def place(self, first, second):
        return (first, second) if self.axes[0] == "x" else (second, first)

    def where(self, step, side):
        return self.axes[step] + side

    def key(self, *name):
        return (self.index, *name)


class Gather(Quarter):
    def __init__(self, held, *others):
        super().__init__(*others)
        self.held = held

    def at(self, place):
        return self.held.at[place[0], place[1], self.rows]

    def send(self, step, side, first, second, name):
        shift = 3 if side == "+" else 1
        there = ((first + shift) % 4, second) if step == 0 else (first, (second + shift) % 4)
        key = ("g", name, first) if name == "last" else self.key("g", name, first)
        self.links.send(
            key, self.at(self.place(first, second)), self.at(self.place(*there)),
            self.where(step, side),
        )

    def arrived(self, name, d, count=1):
        rows = self.rows.size
        self.links.arrived(self.key("g", name, d), self.held.at[0, 0, pl.ds(0, count * rows)])

    def spread(self, d):
        for side in "+-":
            self.send(1, side, d, 0, "spread")

    def pass_on(self, d):
        self.arrived("spread", d, 2)
        self.send(1, self.side, d, 3 if self.side == "+" else 1, "last")

    def own(self):
        for side in "+-":
            self.send(0, side, 0, 0, "own")
        two_away = self.at(self.place(2, 0))
        self.links.send(self.key("g", "far"), self.at(self.place(0, 0)), two_away, (self.axes[0], 2))
        self.spread(0)

    def near(self):
        self.arrived("own", 0, 2)
        self.spread(3)
        self.spread(1)

    def far(self):
        self.links.arrived(self.key("g", "far"), self.at(self.place(2, 0)))
        self.spread(2)


class Sum(Quarter):
    def __init__(self, part, far1, near1, near2, *others):
        super().__init__(*others)
        self.part, self.far1, self.near1, self.near2 = part, far1, near1, near2
        self.near, self.other, self.opposite = (1, 3, "-") if self.side == "+" else (3, 1, "+")

    def at(self, first, second):
        i, j = self.place(first, second)
        return self.part.at[i, j, self.rows]

    def load(self, first, second):
        i, j = self.place(first, second)
        return f32(self.part[i, j, self.rows, :])

    def store(self, first, second, value):
        i, j = self.place(first, second)
        self.part[i, j, self.rows, :] = value.astype(BF16)

    def slot(self, side):
        return 0 if side == "+" else 1

    def forward(self, d):
        self.links.send(self.key("s", "far", d), self.at(d, 2), self.far1.at[self.index, d], self.where(1, self.side))

    def direct(self, d):
        there = self.near1.at[self.index, self.slot(self.opposite), d]
        self.links.send(self.key("s", "near", d), self.at(d, self.other), there, self.where(1, self.opposite))

    def joined(self, d):
        here = self.far1.at[self.index, d]
        self.links.arrived(self.key("s", "far", d), here)
        self.store(d, self.near, self.load(d, self.near) + f32(here[...]))
        there = self.near1.at[self.index, self.slot(self.side), d]
        self.links.send(self.key("s", "near", d), self.at(d, self.near), there, self.where(1, self.side))

    def first_sum(self, d):
        self.links.arrived(self.key("s", "near", d), self.near1.at[self.index, :, d])
        total = self.load(d, 0) + f32(self.near1[self.index, 0, d]) + f32(self.near1[self.index, 1, d])
        if d:
            self.store(d, 0, total)
            there = self.near2.at[self.index, d - 1]
            self.links.send(self.key("s", "near2"), self.at(d, 0), there, (self.axes[0], d))
        else:
            self.own_sum = total

    def result(self):
        self.links.arrived(self.key("s", "near2"), self.near2.at[self.index])
        total = self.own_sum
        for n in range(3):
            total = total + f32(self.near2[self.index, n])
        return total


class PlaneSum:
    def __init__(self, links, index, part, first, staged, second, y):
        self.links, self.index, self.part, self.y = links, index, part, y
        self.first, self.staged, self.second = first, staged, second
        step = part.shape[2] // 4
        self.a, self.b = pl.ds(2 * index * step, step), pl.ds((2 * index + 1) * step, step)

    def start(self):
        for n, d in enumerate((2, 1, 3)):
            self.links.send(
                ("p1a", self.index), self.part.at[:, (self.y + d) % 4, self.a], self.first.at[self.index, 0, n], ("y", d)
            )
            self.links.send(("p1b", self.index), self.part.at[d, :, self.b], self.first.at[self.index, 1, n], ("x", d))

    def second_step(self):
        totals = f32(self.part[:, pl.ds(self.y, 1), self.a, :][:, 0]), f32(self.part[0, :, self.b, :])
        for kind in range(2):
            total = totals[kind]
            self.links.arrived(("p1" + "ab"[kind], self.index), self.first.at[self.index, kind])
            for n in range(3):
                total = total + f32(self.first[self.index, kind, n])
            self.staged[self.index, kind] = total.astype(BF16)
            for n, d in enumerate((2, 1, 3)):
                other = d if kind == 0 else (self.y + d) % 4
                self.links.send(
                    ("p2" + "ab"[kind], self.index), self.staged.at[self.index, kind, other],
                    self.second.at[self.index, kind, n], ("xy"[kind], d),
                )

    def result(self):
        out = []
        for kind in range(2):
            total = f32(self.staged[self.index, 0, 0]) if kind == 0 else f32(self.staged[self.index, 1, self.y])
            self.links.arrived(("p2" + "ab"[kind], self.index), self.second.at[self.index, kind])
            for n in range(3):
                total = total + f32(self.second[self.index, kind, n])
            out.append(total)
        return out


def column_of(line):
    count = line.shape[1]
    shape = (count, count)
    diagonal = lax.broadcasted_iota(jnp.int32, shape, 0) == lax.broadcasted_iota(jnp.int32, shape, 1)
    return jnp.sum(jnp.where(diagonal, line, 0.0), axis=1, keepdims=True)


def attend(queries, keys, values, lengths, wait, index):
    width = queries.shape[1]
    heads = width // HD
    step = 16
    cache = keys.shape[1]
    own = lax.broadcasted_iota(jnp.int32, (heads * step, cache), 0) % step
    position = f32(lax.broadcasted_iota(jnp.int32, (heads * step, cache), 1))
    half_blocks = queries.shape[0] // step // 2
    blocks = range(index * half_blocks, (index + 1) * half_blocks)
    if index:
        wait("k", index)
    every = []
    for n in blocks:
        rows = slice(n * step, (n + 1) * step)
        query = queries[rows, :]
        query = jnp.concatenate([query[:, h * HD:(h + 1) * HD] for h in range(heads)], axis=0)
        every.append(lax.dot_general(
            query, keys[rows].reshape(step * cache, HD), (((1,), (1,)), ((), ())), preferred_element_type=F32
        ))
    spread = []
    for n, products in zip(blocks, every):
        scores = products[:, 0:cache]
        for r in range(1, step):
            scores = jnp.where(own == r, products[:, r * cache:(r + 1) * cache], scores)
        scores = scores * HD ** (-0.5)
        length = jnp.concatenate([lengths[n * step:(n + 1) * step]] * heads, axis=0)
        scores = jnp.where(position < length, scores, -1e30)
        exp_scores = jnp.exp(scores - jnp.max(scores, axis=1, keepdims=True))
        weights = exp_scores / jnp.sum(exp_scores, axis=1, keepdims=True)
        spread.append(jnp.concatenate([jnp.where(own == r, weights, 0.0).astype(BF16) for r in range(step)], axis=1))
    wait("v", index)
    out = []
    for n, weights in zip(blocks, spread):
        rows = slice(n * step, (n + 1) * step)
        combined = jnp.dot(weights, values[rows].reshape(step * cache, HD), preferred_element_type=F32).astype(BF16)
        out.append(jnp.concatenate([combined[h * step:(h + 1) * step] for h in range(heads)], axis=1))
    return jnp.concatenate(out, axis=0)


def kernel(
    queries, keys_hbm, values_hbm, lengths, wo_hbm, res_hbm, gain, expert_ids, gate_weights, wg_hbm, wu_hbm, wd_hbm, out,
    keys, values, wo, wg, wu, wd, res,
    part1, first1, second1, staged1,
    part2, far1, near1, near2,
    held, to_send, landed, back, returned, rows_f32, acc_gate, acc_up, squares, act,
    load_sem, send_sem, recv_sem,
):
    group = lax.axis_index("dp")
    tensor = lax.axis_index("tensor")
    x, y = tensor // 4, tensor % 4
    row_count, share = out.shape
    wide = 4 * share

    def at(i, j):
        return ((x + i) % 4) * 4 + (y + j) % 4

    to = {}
    for d in (1, 2, 3):
        to["x", d] = (group, at(d, 0))
        to["y", d] = (group, at(0, d))
    z, core = group // 2, group % 2
    for k in range(1, 8):
        to[k] = (((z + k // 2) % 4) * 2 + (core + k) % 2, tensor)
    barrier = pltpu.get_barrier_semaphore()
    for where in to:
        pl.semaphore_signal(barrier, inc=1, device_id=to[where], device_id_type=pl.DeviceIdType.MESH)
    peers = len(to)
    for name in ("x", "y"):
        to[name + "+"], to[name + "-"] = to[name, 1], to[name, 3]
    links = Links(send_sem, recv_sem, to)

    loads = {}

    def load(key, src, dst):
        pltpu.make_async_copy(src, dst, load_sem.at[loads.setdefault(key, len(loads))]).start()

    def wait(key, whole):
        pltpu.make_async_copy(whole, whole, load_sem.at[loads[key]]).wait()

    def columns(i):
        return pl.ds(pl.multiple_of(((x + i) % 4) * wide, 128), wide)

    def block_rows(i, j):
        return pl.ds(pl.multiple_of(i * wide + ((y + j) % 4) * share, 128), share)

    def block(j):
        return pl.ds(pl.multiple_of(((y + j) % 4) * share, 128), share)

    def cached(name, index):
        array = keys if name == "k" else values
        return array.at[pl.ds(index * half, half)]

    def load_cache(index):
        for name, array in (("k", keys_hbm), ("v", values_hbm)):
            load((name, index), array.at[pl.ds(index * half, half), 0], cached(name, index))

    def wait_cache(name, index):
        wait((name, index), cached(name, index))

    half = row_count // 2
    load_cache(0)
    wait_cache("k", 0)
    for i in range(4):
        load("wo", wo_hbm.at[:, columns(i)], wo.at[i])
    load_cache(1)
    load("res", res_hbm.at[:, pl.ds(pl.multiple_of(tensor * share, 128), share)], res)

    length_column = column_of(f32(lengths[...]))
    halves = [PlaneSum(links, index, part1, first1, staged1, second1, y) for index in range(2)]

    def project(attended, index):
        for i in (2, 1, 3, 0):
            product = jnp.dot(attended, wo[i], preferred_element_type=F32).astype(BF16)
            for j in range(4):
                part1[i, j, index * half:(index + 1) * half, :] = product[:, j * share:(j + 1) * share]

    attended = attend(queries, keys, values, length_column, wait_cache, 0)
    wait("wo", wo)
    project(attended, 0)
    pl.semaphore_wait(barrier, peers)
    halves[0].start()
    project(attend(queries, keys, values, length_column, wait_cache, 1), 1)
    halves[1].start()

    for i in (0, 3, 1, 2):
        load("wg", wg_hbm.at[0, columns(i)], wg.at[pl.ds(i * wide, wide)])
        load("wu", wu_hbm.at[0, columns(i)], wu.at[pl.ds(i * wide, wide)])
    for i in (2, 1, 3, 0):
        load("wd", wd_hbm.at[0, :, columns(i)], wd.at[i])

    def slot_tables():
        slots = 8 * PAD
        ids = expert_ids[...]
        relative = f32((ids // 2 - z + 4) % 4 * 2 + (ids + core) % 2)
        column = lax.broadcasted_iota(jnp.int32, (row_count, slots), 1)
        expert = f32(column // PAD)
        first = jnp.where(column_of(relative[0:1]) == expert, 1.0, 0.0)
        second = jnp.where(column_of(relative[1:2]) == expert, 1.0, 0.0)
        named = first + second
        earlier = jnp.where(
            lax.broadcasted_iota(jnp.int32, (row_count, row_count), 1)
            < lax.broadcasted_iota(jnp.int32, (row_count, row_count), 0),
            1.0,
            0.0,
        )
        rank = jnp.dot(earlier.astype(BF16), named.astype(BF16), preferred_element_type=F32)
        place = jnp.where(rank == f32(column % PAD), 1.0, 0.0)
        acc_gate[...] = jnp.zeros_like(acc_gate)
        acc_up[...] = jnp.zeros_like(acc_up)
        squares[...] = jnp.zeros_like(squares)
        return [(rows * place).astype(BF16) for rows in (first, second, named)]

    first, second, chosen = slot_tables()
    first_weight, second_weight = column_of(gate_weights[0:1]), column_of(gate_weights[1:2])
    for each in halves:
        each.second_step()
    summed = jnp.concatenate(halves[0].result() + halves[1].result(), axis=0)
    wait("res", res)
    hidden = summed + f32(res[...])
    picked = lax.dot_general(
        chosen, hidden.astype(BF16), (((0,), (0,)), ((), ())), preferred_element_type=F32
    )
    to_send[...] = picked.astype(BF16).reshape(8, PAD, share)

    for k in (2, 3, 6, 7, 1, 4, 5):
        links.send("d", to_send.at[k], landed.at[k - 1], k)
    quarter = 2 * CAP
    gathers = [
        Gather(held, links, index, quarter, axes, side)
        for index, (axes, side) in enumerate((("xy", "+"), ("yx", "+"), ("yx", "-"), ("xy", "-")))
    ]

    rows_f32[0:CAP, :] = f32(to_send[0])[:CAP]
    links.arrived("d", landed)
    for k in range(1, 8):
        rows_f32[k * CAP:(k + 1) * CAP, :] = f32(landed[k - 1])[:CAP]
    held[0, 0] = rows_f32[...].astype(BF16)

    def consume(i, j):
        values_f32 = f32(held[i, j])
        square = values_f32 * values_f32
        folded = square[:, 0:128]
        for c in range(1, share // 128):
            folded = folded + square[:, c * 128:(c + 1) * 128]
        squares[...] += folded
        scaled = (values_f32 * f32(gain[0:1, pl.ds(pl.multiple_of(at(i, j) * share, 128), share)])).astype(BF16)
        acc_gate[...] += jnp.dot(scaled, wg[block_rows(i, j), :], preferred_element_type=F32)
        acc_up[...] += jnp.dot(scaled, wu[block_rows(i, j), :], preferred_element_type=F32)

    for each in gathers:
        each.own()
    wait("wg", wg)
    wait("wu", wu)
    consume(0, 0)
    for each in gathers:
        each.near()
    for each in gathers:
        each.pass_on(0)
    for each in gathers:
        each.far()
    for i, j in ((3, 0), (0, 3), (1, 0), (0, 1)):
        consume(i, j)
    for d in (3, 1):
        for each in gathers:
            each.pass_on(d)
    for i, j in ((3, 3), (1, 3), (3, 1), (1, 1)):
        consume(i, j)
    for each in gathers:
        each.pass_on(2)
    for d in (0, 3, 1):
        links.arrived(("g", "last", d), held.at[d, 2])
        consume(d, 2)
        consume(2, d)
    links.arrived(("g", "last", 2), held.at[2, 2])
    consume(2, 2)

    mean = jnp.sum(squares[...], axis=1, keepdims=True) * (1.0 / (16 * share))
    inverse = lax.rsqrt(mean + EPSILON)
    gate = acc_gate[...] * inverse
    up = acc_up[...] * inverse
    act[...] = (gate / (1.0 + jnp.exp(-gate)) * up).astype(BF16)
    wait("wd", wd)

    def down(i, j):
        part2[i, j] = jnp.dot(act[...], wd[i, :, block(j)], preferred_element_type=F32).astype(BF16)

    sums = [
        Sum(part2, far1, near1, near2, links, index, quarter, axes, side)
        for index, (axes, side) in enumerate((("yx", "-"), ("yx", "+"), ("xy", "+"), ("xy", "-")))
    ]
    for i, j in ORDER:
        down(i, j)
        for each in sums:
            d, along = each.place(i, j)
            if along == 2:
                each.forward(d)
    for d in (2, 1, 3, 0):
        for each in sums:
            each.joined(d)
            each.direct(d)
    for d in (2, 3, 1, 0):
        for each in sums:
            each.first_sum(d)

    empty = jnp.zeros((PAD - CAP, share), F32)

    def give_back(each):
        total = each.result()
        for k in (2 * each.index, 2 * each.index + 1):
            first_row = (k % 2) * CAP
            slot = jnp.concatenate([total[first_row:first_row + CAP], empty], axis=0).astype(BF16)
            if k == 0:
                returned[0] = slot
            else:
                back[k] = slot
                links.send("b", back.at[k], returned.at[k], (4 - k // 2) % 4 * 2 + k % 2)

    for index in (2, 3, 1, 0):
        give_back(sums[index])
    links.finish(wg)
    links.arrived("b", returned.at[pl.ds(1, 7)])
    results = returned[...].reshape(8 * PAD, share)
    layer_out = (
        hidden
        + first_weight * jnp.dot(first, results, preferred_element_type=F32)
        + second_weight * jnp.dot(second, results, preferred_element_type=F32)
    )
    out[...] = layer_out.astype(out.dtype)


def local(
    queries, key_cache, value_cache, lengths, out_proj, residual, norm_gain, expert_ids, gate_weights,
    w_gate, w_up, w_down,
):
    rows, share = queries.shape
    cache = key_cache.shape[2]
    hidden_units = w_gate.shape[2]
    slots = 8 * CAP
    vmem = pl.BlockSpec(memory_space=pltpu.VMEM)
    hbm = pl.BlockSpec(memory_space=pl.ANY)
    quarter = slots // 4
    step = rows // 4

    return pl.pallas_call(
        kernel,
        out_shape=jax.ShapeDtypeStruct((rows, share), BF16),
        in_specs=[vmem, hbm, hbm, vmem, hbm, hbm, vmem, vmem, vmem, hbm, hbm, hbm],
        out_specs=vmem,
        scratch_shapes=[
            pltpu.VMEM((rows, cache, HD), BF16),
            pltpu.VMEM((rows, cache, HD), BF16),
            pltpu.VMEM((4, share, 4 * share), BF16),
            pltpu.VMEM((16 * share, hidden_units), BF16),
            pltpu.VMEM((16 * share, hidden_units), BF16),
            pltpu.VMEM((4, hidden_units, 4 * share), BF16),
            pltpu.VMEM((rows, share), BF16),
            pltpu.VMEM((4, 4, rows, share), BF16),
            pltpu.VMEM((2, 2, 3, 4, step, share), BF16),
            pltpu.VMEM((2, 2, 3, step, share), BF16),
            pltpu.VMEM((2, 2, 4, step, share), BF16),
            pltpu.VMEM((4, 4, slots, share), BF16),
            pltpu.VMEM((4, 4, quarter, share), BF16),
            pltpu.VMEM((4, 2, 4, quarter, share), BF16),
            pltpu.VMEM((4, 3, quarter, share), BF16),
            pltpu.VMEM((4, 4, slots, share), BF16),
            pltpu.VMEM((8, PAD, share), BF16),
            pltpu.VMEM((7, PAD, share), BF16),
            pltpu.VMEM((8, PAD, share), BF16),
            pltpu.VMEM((8, PAD, share), BF16),
            pltpu.VMEM((slots, share), F32),
            pltpu.VMEM((slots, hidden_units), F32),
            pltpu.VMEM((slots, hidden_units), F32),
            pltpu.VMEM((slots, 128), F32),
            pltpu.VMEM((slots, hidden_units), BF16),
            pltpu.SemaphoreType.DMA((10,)),
            pltpu.SemaphoreType.DMA((1,)),
            pltpu.SemaphoreType.DMA((N_SEMS,)),
        ],
        compiler_params=pltpu.CompilerParams(
            collective_id=0, has_side_effects=True, vmem_limit_bytes=56 * 1024 * 1024
        ),
    )(
        queries, key_cache, value_cache, lengths.reshape(1, rows), out_proj, residual, norm_gain.reshape(1, 16 * share),
        expert_ids.T, gate_weights.T, w_gate, w_up, w_down,
    )


def solution(mesh):
    placed = (
        P("dp", "tensor"),
        P("dp", "tensor", None, None),
        P("dp", "tensor", None, None),
        P("dp"),
        P("tensor", None),
        P("dp", None),
        P(),
        P("dp", None),
        P("dp", None),
        P("dp", None, "tensor"),
        P("dp", None, "tensor"),
        P("dp", "tensor", None),
    )
    return jax.shard_map(
        local, mesh=mesh, in_specs=placed, out_specs=P("dp", "tensor"), check_vma=False
    )
```

```python
import math

import jax
import jax.numpy as jnp
from jax import lax
from jax.experimental import pallas as pl
from jax.experimental.pallas import tpu as pltpu
from jax.sharding import PartitionSpec as P

HD = 128
CAP = 24
PAD = 32
EPSILON = 1e-05
F32 = jnp.float32
BF16 = jnp.bfloat16
N_SEMS = 8 + 28 + 36 + 1 + 1

ORDER = (
    (2, 2), (1, 2), (3, 2), (2, 1), (2, 3), (1, 1), (1, 3), (3, 1), (3, 3),
    (2, 0), (0, 2), (1, 0), (3, 0), (0, 1), (0, 3), (0, 0),
)


class Links:
    def __init__(self, send_sem, recv_sem, to):
        self.send_sem, self.recv_sem, self.to = send_sem, recv_sem, to
        self.sent = 0
        self.numbers = {}

    def copy(self, key, src, dst, where):
        number = self.numbers.setdefault(key, len(self.numbers))
        return pltpu.make_async_remote_copy(
            src_ref=src,
            dst_ref=dst,
            send_sem=self.send_sem.at[0],
            recv_sem=self.recv_sem.at[number],
            device_id=self.to[where],
            device_id_type=pl.DeviceIdType.MESH,
        )

    def send(self, key, src, dst, where):
        self.copy(key, src, dst, where).start()
        self.sent += math.prod(src.shape)

    def arrived(self, key, dst):
        self.copy(key, dst, dst, "x+").wait_recv()

    def finish(self, space):
        space = space.at[pl.ds(0, self.sent // space.shape[1])]
        self.copy(next(iter(self.numbers)), space, space, "x+").wait_send()


def f32(value):
    return value.astype(F32)


class Quarter:
    def __init__(self, links, index, rows, axes, side):
        self.links, self.index, self.axes, self.side = links, index, axes, side
        self.rows = pl.ds(index * rows, rows)

    def place(self, first, second):
        return (first, second) if self.axes[0] == "x" else (second, first)

    def where(self, step, side):
        return self.axes[step] + side

    def key(self, *name):
        return (self.index, *name)


class Gather(Quarter):
    def __init__(self, held, *others):
        super().__init__(*others)
        self.held = held

    def at(self, place):
        return self.held.at[place[0], place[1], self.rows]

    def send(self, step, side, first, second, name):
        shift = 3 if side == "+" else 1
        there = ((first + shift) % 4, second) if step == 0 else (first, (second + shift) % 4)
        key = ("g", name, first) if name == "last" else self.key("g", name, first)
        self.links.send(
            key, self.at(self.place(first, second)), self.at(self.place(*there)),
            self.where(step, side),
        )

    def arrived(self, name, d, count=1):
        rows = self.rows.size
        self.links.arrived(self.key("g", name, d), self.held.at[0, 0, pl.ds(0, count * rows)])

    def spread(self, d):
        for side in "+-":
            self.send(1, side, d, 0, "spread")

    def pass_on(self, d):
        self.arrived("spread", d, 2)
        self.send(1, self.side, d, 3 if self.side == "+" else 1, "last")

    def own(self):
        for side in "+-":
            self.send(0, side, 0, 0, "own")
        two_away = self.at(self.place(2, 0))
        self.links.send(self.key("g", "far"), self.at(self.place(0, 0)), two_away, (self.axes[0], 2))
        self.spread(0)

    def near(self):
        self.arrived("own", 0, 2)
        self.spread(3)
        self.spread(1)

    def far(self):
        self.links.arrived(self.key("g", "far"), self.at(self.place(2, 0)))
        self.spread(2)


class Sum(Quarter):
    def __init__(self, part, far1, near1, near2, *others):
        super().__init__(*others)
        self.part, self.far1, self.near1, self.near2 = part, far1, near1, near2
        self.near, self.other, self.opposite = (1, 3, "-") if self.side == "+" else (3, 1, "+")

    def at(self, first, second):
        i, j = self.place(first, second)
        return self.part.at[i, j, self.rows]

    def load(self, first, second):
        i, j = self.place(first, second)
        return f32(self.part[i, j, self.rows, :])

    def store(self, first, second, value):
        i, j = self.place(first, second)
        self.part[i, j, self.rows, :] = value.astype(BF16)

    def slot(self, side):
        return 0 if side == "+" else 1

    def forward(self, d):
        self.links.send(self.key("s", "far", d), self.at(d, 2), self.far1.at[self.index, d], self.where(1, self.side))

    def direct(self, d):
        there = self.near1.at[self.index, self.slot(self.opposite), d]
        self.links.send(self.key("s", "near", d), self.at(d, self.other), there, self.where(1, self.opposite))

    def joined(self, d):
        here = self.far1.at[self.index, d]
        self.links.arrived(self.key("s", "far", d), here)
        self.store(d, self.near, self.load(d, self.near) + f32(here[...]))
        there = self.near1.at[self.index, self.slot(self.side), d]
        self.links.send(self.key("s", "near", d), self.at(d, self.near), there, self.where(1, self.side))

    def first_sum(self, d):
        self.links.arrived(self.key("s", "near", d), self.near1.at[self.index, :, d])
        total = self.load(d, 0) + f32(self.near1[self.index, 0, d]) + f32(self.near1[self.index, 1, d])
        if d:
            self.store(d, 0, total)
            there = self.near2.at[self.index, d - 1]
            self.links.send(self.key("s", "near2"), self.at(d, 0), there, (self.axes[0], d))
        else:
            self.own_sum = total

    def result(self):
        self.links.arrived(self.key("s", "near2"), self.near2.at[self.index])
        total = self.own_sum
        for n in range(3):
            total = total + f32(self.near2[self.index, n])
        return total


class PlaneSum:
    def __init__(self, links, index, part, first, staged, second, y):
        self.links, self.index, self.part, self.y = links, index, part, y
        self.first, self.staged, self.second = first, staged, second
        step = part.shape[2] // 4
        self.a, self.b = pl.ds(2 * index * step, step), pl.ds((2 * index + 1) * step, step)

    def start(self):
        for n, d in enumerate((2, 1, 3)):
            self.links.send(
                ("p1a", self.index), self.part.at[:, (self.y + d) % 4, self.a], self.first.at[self.index, 0, n], ("y", d)
            )
            self.links.send(("p1b", self.index), self.part.at[d, :, self.b], self.first.at[self.index, 1, n], ("x", d))

    def second_step(self):
        totals = f32(self.part[:, pl.ds(self.y, 1), self.a, :][:, 0]), f32(self.part[0, :, self.b, :])
        for kind in range(2):
            total = totals[kind]
            self.links.arrived(("p1" + "ab"[kind], self.index), self.first.at[self.index, kind])
            for n in range(3):
                total = total + f32(self.first[self.index, kind, n])
            self.staged[self.index, kind] = total.astype(BF16)
            for n, d in enumerate((2, 1, 3)):
                other = d if kind == 0 else (self.y + d) % 4
                self.links.send(
                    ("p2" + "ab"[kind], self.index), self.staged.at[self.index, kind, other],
                    self.second.at[self.index, kind, n], ("xy"[kind], d),
                )

    def result(self):
        out = []
        for kind in range(2):
            total = f32(self.staged[self.index, 0, 0]) if kind == 0 else f32(self.staged[self.index, 1, self.y])
            self.links.arrived(("p2" + "ab"[kind], self.index), self.second.at[self.index, kind])
            for n in range(3):
                total = total + f32(self.second[self.index, kind, n])
            out.append(total)
        return out


def column_of(line):
    count = line.shape[1]
    shape = (count, count)
    diagonal = lax.broadcasted_iota(jnp.int32, shape, 0) == lax.broadcasted_iota(jnp.int32, shape, 1)
    return jnp.sum(jnp.where(diagonal, line, 0.0), axis=1, keepdims=True)


def attend(queries, keys, values, lengths, wait, index):
    width = queries.shape[1]
    heads = width // HD
    step = 16
    cache = keys.shape[1]
    own = lax.broadcasted_iota(jnp.int32, (heads * step, cache), 0) % step
    position = f32(lax.broadcasted_iota(jnp.int32, (heads * step, cache), 1))
    half_blocks = queries.shape[0] // step // 2
    blocks = range(index * half_blocks, (index + 1) * half_blocks)
    if index:
        wait("k", index)
    every = []
    for n in blocks:
        rows = slice(n * step, (n + 1) * step)
        query = queries[rows, :]
        query = jnp.concatenate([query[:, h * HD:(h + 1) * HD] for h in range(heads)], axis=0)
        every.append(lax.dot_general(
            query, keys[rows].reshape(step * cache, HD), (((1,), (1,)), ((), ())), preferred_element_type=F32
        ))
    spread = []
    for n, products in zip(blocks, every):
        scores = products[:, 0:cache]
        for r in range(1, step):
            scores = jnp.where(own == r, products[:, r * cache:(r + 1) * cache], scores)
        scores = scores * HD ** (-0.5)
        length = jnp.concatenate([lengths[n * step:(n + 1) * step]] * heads, axis=0)
        scores = jnp.where(position < length, scores, -1e30)
        exp_scores = jnp.exp(scores - jnp.max(scores, axis=1, keepdims=True))
        weights = exp_scores / jnp.sum(exp_scores, axis=1, keepdims=True)
        spread.append(jnp.concatenate([jnp.where(own == r, weights, 0.0).astype(BF16) for r in range(step)], axis=1))
    wait("v", index)
    out = []
    for n, weights in zip(blocks, spread):
        rows = slice(n * step, (n + 1) * step)
        combined = jnp.dot(weights, values[rows].reshape(step * cache, HD), preferred_element_type=F32).astype(BF16)
        out.append(jnp.concatenate([combined[h * step:(h + 1) * step] for h in range(heads)], axis=1))
    return jnp.concatenate(out, axis=0)


def kernel(
    queries, keys_hbm, values_hbm, lengths, wo_hbm, res_hbm, gain, expert_ids, gate_weights, wg_hbm, wu_hbm, wd_hbm, out,
    keys, values, wo, wg, wu, wd, res,
    part1, first1, second1, staged1,
    part2, far1, near1, near2,
    held, to_send, landed, back, returned, rows_f32, acc_gate, acc_up, squares, act,
    load_sem, send_sem, recv_sem,
):
    group = lax.axis_index("dp")
    tensor = lax.axis_index("tensor")
    x, y = tensor // 4, tensor % 4
    row_count, share = out.shape
    wide = 4 * share

    def at(i, j):
        return ((x + i) % 4) * 4 + (y + j) % 4

    to = {}
    for d in (1, 2, 3):
        to["x", d] = (group, at(d, 0))
        to["y", d] = (group, at(0, d))
    z, core = group // 2, group % 2
    for k in range(1, 8):
        to[k] = (((z + k // 2) % 4) * 2 + (core + k) % 2, tensor)
    barrier = pltpu.get_barrier_semaphore()
    for where in to:
        pl.semaphore_signal(barrier, inc=1, device_id=to[where], device_id_type=pl.DeviceIdType.MESH)
    peers = len(to)
    for name in ("x", "y"):
        to[name + "+"], to[name + "-"] = to[name, 1], to[name, 3]
    links = Links(send_sem, recv_sem, to)

    loads = {}

    def load(key, src, dst):
        pltpu.make_async_copy(src, dst, load_sem.at[loads.setdefault(key, len(loads))]).start()

    def wait(key, whole):
        pltpu.make_async_copy(whole, whole, load_sem.at[loads[key]]).wait()

    def columns(i):
        return pl.ds(pl.multiple_of(((x + i) % 4) * wide, 128), wide)

    def block_rows(i, j):
        return pl.ds(pl.multiple_of(i * wide + ((y + j) % 4) * share, 128), share)

    def block(j):
        return pl.ds(pl.multiple_of(((y + j) % 4) * share, 128), share)

    def cached(name, index):
        array = keys if name == "k" else values
        return array.at[pl.ds(index * half, half)]

    def load_cache(index):
        for name, array in (("k", keys_hbm), ("v", values_hbm)):
            load((name, index), array.at[pl.ds(index * half, half), 0], cached(name, index))

    def wait_cache(name, index):
        wait((name, index), cached(name, index))

    half = row_count // 2
    load_cache(0)
    wait_cache("k", 0)
    for i in range(4):
        load("wo", wo_hbm.at[:, columns(i)], wo.at[i])
    load_cache(1)
    load("res", res_hbm.at[:, pl.ds(pl.multiple_of(tensor * share, 128), share)], res)

    length_column = column_of(f32(lengths[...]))
    halves = [PlaneSum(links, index, part1, first1, staged1, second1, y) for index in range(2)]

    def project(attended, index):
        for i in (2, 1, 3, 0):
            product = jnp.dot(attended, wo[i], preferred_element_type=F32).astype(BF16)
            for j in range(4):
                part1[i, j, index * half:(index + 1) * half, :] = product[:, j * share:(j + 1) * share]

    attended = attend(queries, keys, values, length_column, wait_cache, 0)
    wait("wo", wo)
    project(attended, 0)
    pl.semaphore_wait(barrier, peers)
    halves[0].start()
    project(attend(queries, keys, values, length_column, wait_cache, 1), 1)
    halves[1].start()

    for i in (0, 3, 1, 2):
        load("wg", wg_hbm.at[0, columns(i)], wg.at[pl.ds(i * wide, wide)])
        load("wu", wu_hbm.at[0, columns(i)], wu.at[pl.ds(i * wide, wide)])
    for i in (2, 1, 3, 0):
        load("wd", wd_hbm.at[0, :, columns(i)], wd.at[i])

    def slot_tables():
        slots = 8 * PAD
        ids = expert_ids[...]
        relative = f32((ids // 2 - z + 4) % 4 * 2 + (ids + core) % 2)
        column = lax.broadcasted_iota(jnp.int32, (row_count, slots), 1)
        expert = f32(column // PAD)
        first = jnp.where(column_of(relative[0:1]) == expert, 1.0, 0.0)
        second = jnp.where(column_of(relative[1:2]) == expert, 1.0, 0.0)
        named = first + second
        earlier = jnp.where(
            lax.broadcasted_iota(jnp.int32, (row_count, row_count), 1)
            < lax.broadcasted_iota(jnp.int32, (row_count, row_count), 0),
            1.0,
            0.0,
        )
        rank = jnp.dot(earlier.astype(BF16), named.astype(BF16), preferred_element_type=F32)
        place = jnp.where(rank == f32(column % PAD), 1.0, 0.0)
        acc_gate[...] = jnp.zeros_like(acc_gate)
        acc_up[...] = jnp.zeros_like(acc_up)
        squares[...] = jnp.zeros_like(squares)
        return [(rows * place).astype(BF16) for rows in (first, second, named)]

    first, second, chosen = slot_tables()
    first_weight, second_weight = column_of(gate_weights[0:1]), column_of(gate_weights[1:2])
    for each in halves:
        each.second_step()
    summed = jnp.concatenate(halves[0].result() + halves[1].result(), axis=0)
    wait("res", res)
    hidden = summed + f32(res[...])
    picked = lax.dot_general(
        chosen, hidden.astype(BF16), (((0,), (0,)), ((), ())), preferred_element_type=F32
    )
    to_send[...] = picked.astype(BF16).reshape(8, PAD, share)

    for k in (4, 5, 2, 3, 6, 7, 1):
        links.send("d", to_send.at[k], landed.at[k - 1], k)
    quarter = 2 * CAP
    gathers = [
        Gather(held, links, index, quarter, axes, side)
        for index, (axes, side) in enumerate((("xy", "+"), ("yx", "+"), ("yx", "-"), ("xy", "-")))
    ]

    rows_f32[0:CAP, :] = f32(to_send[0])[:CAP]
    links.arrived("d", landed)
    for k in range(1, 8):
        rows_f32[k * CAP:(k + 1) * CAP, :] = f32(landed[k - 1])[:CAP]
    held[0, 0] = rows_f32[...].astype(BF16)

    def consume(i, j):
        values_f32 = f32(held[i, j])
        square = values_f32 * values_f32
        folded = square[:, 0:128]
        for c in range(1, share // 128):
            folded = folded + square[:, c * 128:(c + 1) * 128]
        squares[...] += folded
        scaled = (values_f32 * f32(gain[0:1, pl.ds(pl.multiple_of(at(i, j) * share, 128), share)])).astype(BF16)
        acc_gate[...] += jnp.dot(scaled, wg[block_rows(i, j), :], preferred_element_type=F32)
        acc_up[...] += jnp.dot(scaled, wu[block_rows(i, j), :], preferred_element_type=F32)

    for each in gathers:
        each.own()
    wait("wg", wg)
    wait("wu", wu)
    consume(0, 0)
    for each in gathers:
        each.near()
    for each in gathers:
        each.pass_on(0)
    for each in gathers:
        each.far()
    for i, j in ((3, 0), (0, 3), (1, 0), (0, 1)):
        consume(i, j)
    for d in (3, 1):
        for each in gathers:
            each.pass_on(d)
    for i, j in ((3, 3), (1, 3), (3, 1), (1, 1)):
        consume(i, j)
    for each in gathers:
        each.pass_on(2)
    for d in (0, 3, 1):
        links.arrived(("g", "last", d), held.at[d, 2])
        consume(d, 2)
        consume(2, d)
    links.arrived(("g", "last", 2), held.at[2, 2])
    consume(2, 2)

    mean = jnp.sum(squares[...], axis=1, keepdims=True) * (1.0 / (16 * share))
    inverse = lax.rsqrt(mean + EPSILON)
    gate = acc_gate[...] * inverse
    up = acc_up[...] * inverse
    act[...] = (gate / (1.0 + jnp.exp(-gate)) * up).astype(BF16)
    wait("wd", wd)

    def down(i, j):
        part2[i, j] = jnp.dot(act[...], wd[i, :, block(j)], preferred_element_type=F32).astype(BF16)

    sums = [
        Sum(part2, far1, near1, near2, links, index, quarter, axes, side)
        for index, (axes, side) in enumerate((("yx", "-"), ("yx", "+"), ("xy", "+"), ("xy", "-")))
    ]
    for i, j in ORDER:
        down(i, j)
        for each in sums:
            d, along = each.place(i, j)
            if along == 2:
                each.forward(d)
    for d in (2, 1, 3, 0):
        for each in sums:
            each.joined(d)
            each.direct(d)
    for d in (2, 3, 1, 0):
        for each in sums:
            each.first_sum(d)

    empty = jnp.zeros((PAD - CAP, share), F32)

    def give_back(each):
        total = each.result()
        for k in (2 * each.index, 2 * each.index + 1):
            first_row = (k % 2) * CAP
            slot = jnp.concatenate([total[first_row:first_row + CAP], empty], axis=0).astype(BF16)
            if k == 0:
                returned[0] = slot
            else:
                back[k] = slot
                links.send("b", back.at[k], returned.at[k], (4 - k // 2) % 4 * 2 + k % 2)

    for index in (2, 3, 1, 0):
        give_back(sums[index])
    links.finish(wg)
    links.arrived("b", returned.at[pl.ds(1, 7)])
    results = returned[...].reshape(8 * PAD, share)
    layer_out = (
        hidden
        + first_weight * jnp.dot(first, results, preferred_element_type=F32)
        + second_weight * jnp.dot(second, results, preferred_element_type=F32)
    )
    out[...] = layer_out.astype(out.dtype)


def local(
    queries, key_cache, value_cache, lengths, out_proj, residual, norm_gain, expert_ids, gate_weights,
    w_gate, w_up, w_down,
):
    rows, share = queries.shape
    cache = key_cache.shape[2]
    hidden_units = w_gate.shape[2]
    slots = 8 * CAP
    vmem = pl.BlockSpec(memory_space=pltpu.VMEM)
    hbm = pl.BlockSpec(memory_space=pl.ANY)
    quarter = slots // 4
    step = rows // 4

    return pl.pallas_call(
        kernel,
        out_shape=jax.ShapeDtypeStruct((rows, share), BF16),
        in_specs=[vmem, hbm, hbm, vmem, hbm, hbm, vmem, vmem, vmem, hbm, hbm, hbm],
        out_specs=vmem,
        scratch_shapes=[
            pltpu.VMEM((rows, cache, HD), BF16),
            pltpu.VMEM((rows, cache, HD), BF16),
            pltpu.VMEM((4, share, 4 * share), BF16),
            pltpu.VMEM((16 * share, hidden_units), BF16),
            pltpu.VMEM((16 * share, hidden_units), BF16),
            pltpu.VMEM((4, hidden_units, 4 * share), BF16),
            pltpu.VMEM((rows, share), BF16),
            pltpu.VMEM((4, 4, rows, share), BF16),
            pltpu.VMEM((2, 2, 3, 4, step, share), BF16),
            pltpu.VMEM((2, 2, 3, step, share), BF16),
            pltpu.VMEM((2, 2, 4, step, share), BF16),
            pltpu.VMEM((4, 4, slots, share), BF16),
            pltpu.VMEM((4, 4, quarter, share), BF16),
            pltpu.VMEM((4, 2, 4, quarter, share), BF16),
            pltpu.VMEM((4, 3, quarter, share), BF16),
            pltpu.VMEM((4, 4, slots, share), BF16),
            pltpu.VMEM((8, PAD, share), BF16),
            pltpu.VMEM((7, PAD, share), BF16),
            pltpu.VMEM((8, PAD, share), BF16),
            pltpu.VMEM((8, PAD, share), BF16),
            pltpu.VMEM((slots, share), F32),
            pltpu.VMEM((slots, hidden_units), F32),
            pltpu.VMEM((slots, hidden_units), F32),
            pltpu.VMEM((slots, 128), F32),
            pltpu.VMEM((slots, hidden_units), BF16),
            pltpu.SemaphoreType.DMA((10,)),
            pltpu.SemaphoreType.DMA((1,)),
            pltpu.SemaphoreType.DMA((N_SEMS,)),
        ],
        compiler_params=pltpu.CompilerParams(
            collective_id=0, has_side_effects=True, vmem_limit_bytes=56 * 1024 * 1024
        ),
    )(
        queries, key_cache, value_cache, lengths.reshape(1, rows), out_proj, residual, norm_gain.reshape(1, 16 * share),
        expert_ids.T, gate_weights.T, w_gate, w_up, w_down,
    )


def solution(mesh):
    placed = (
        P("dp", "tensor"),
        P("dp", "tensor", None, None),
        P("dp", "tensor", None, None),
        P("dp"),
        P("tensor", None),
        P("dp", None),
        P(),
        P("dp", None),
        P("dp", None),
        P("dp", None, "tensor"),
        P("dp", None, "tensor"),
        P("dp", "tensor", None),
    )
    return jax.shard_map(
        local, mesh=mesh, in_specs=placed, out_specs=P("dp", "tensor"), check_vma=False
    )
```

```python
import math

import jax
import jax.numpy as jnp
from jax import lax
from jax.experimental import pallas as pl
from jax.experimental.pallas import tpu as pltpu
from jax.sharding import PartitionSpec as P

HD = 128
CAP = 24
PAD = 32
EPSILON = 1e-05
F32 = jnp.float32
BF16 = jnp.bfloat16
N_SEMS = 8 + 28 + 36 + 2 + 1

ORDER = (
    (2, 2), (1, 2), (3, 2), (2, 1), (2, 3), (1, 1), (1, 3), (3, 1), (3, 3),
    (2, 0), (0, 2), (1, 0), (3, 0), (0, 1), (0, 3), (0, 0),
)


class Links:
    def __init__(self, send_sem, recv_sem, to):
        self.send_sem, self.recv_sem, self.to = send_sem, recv_sem, to
        self.sent = 0
        self.numbers = {}

    def copy(self, key, src, dst, where):
        number = self.numbers.setdefault(key, len(self.numbers))
        return pltpu.make_async_remote_copy(
            src_ref=src,
            dst_ref=dst,
            send_sem=self.send_sem.at[0],
            recv_sem=self.recv_sem.at[number],
            device_id=self.to[where],
            device_id_type=pl.DeviceIdType.MESH,
        )

    def send(self, key, src, dst, where):
        self.copy(key, src, dst, where).start()
        self.sent += math.prod(src.shape)

    def arrived(self, key, dst):
        self.copy(key, dst, dst, "x+").wait_recv()

    def finish(self, space):
        space = space.at[pl.ds(0, self.sent // space.shape[1])]
        self.copy(next(iter(self.numbers)), space, space, "x+").wait_send()


def f32(value):
    return value.astype(F32)


class Quarter:
    def __init__(self, links, index, rows, axes, side):
        self.links, self.index, self.axes, self.side = links, index, axes, side
        self.rows = pl.ds(index * rows, rows)

    def place(self, first, second):
        return (first, second) if self.axes[0] == "x" else (second, first)

    def where(self, step, side):
        return self.axes[step] + side

    def key(self, *name):
        return (self.index, *name)


class Gather(Quarter):
    def __init__(self, held, *others):
        super().__init__(*others)
        self.held = held

    def at(self, place):
        return self.held.at[place[0], place[1], self.rows]

    def send(self, step, side, first, second, name):
        shift = 3 if side == "+" else 1
        there = ((first + shift) % 4, second) if step == 0 else (first, (second + shift) % 4)
        key = ("g", name, first) if name == "last" else self.key("g", name, first)
        self.links.send(
            key, self.at(self.place(first, second)), self.at(self.place(*there)),
            self.where(step, side),
        )

    def arrived(self, name, d, count=1):
        rows = self.rows.size
        self.links.arrived(self.key("g", name, d), self.held.at[0, 0, pl.ds(0, count * rows)])

    def spread(self, d):
        for side in "+-":
            self.send(1, side, d, 0, "spread")

    def pass_on(self, d):
        self.arrived("spread", d, 2)
        self.send(1, self.side, d, 3 if self.side == "+" else 1, "last")

    def own(self):
        for side in "+-":
            self.send(0, side, 0, 0, "own")
        two_away = self.at(self.place(2, 0))
        self.links.send(self.key("g", "far"), self.at(self.place(0, 0)), two_away, (self.axes[0], 2))
        self.spread(0)

    def near(self):
        self.arrived("own", 0, 2)
        self.spread(3)
        self.spread(1)

    def far(self):
        self.links.arrived(self.key("g", "far"), self.at(self.place(2, 0)))
        self.spread(2)


class Sum(Quarter):
    def __init__(self, part, far1, near1, near2, *others):
        super().__init__(*others)
        self.part, self.far1, self.near1, self.near2 = part, far1, near1, near2
        self.near, self.other, self.opposite = (1, 3, "-") if self.side == "+" else (3, 1, "+")

    def at(self, first, second):
        i, j = self.place(first, second)
        return self.part.at[i, j, self.rows]

    def load(self, first, second):
        i, j = self.place(first, second)
        return f32(self.part[i, j, self.rows, :])

    def store(self, first, second, value):
        i, j = self.place(first, second)
        self.part[i, j, self.rows, :] = value.astype(BF16)

    def slot(self, side):
        return 0 if side == "+" else 1

    def forward(self, d):
        self.links.send(self.key("s", "far", d), self.at(d, 2), self.far1.at[self.index, d], self.where(1, self.side))

    def direct(self, d):
        there = self.near1.at[self.index, self.slot(self.opposite), d]
        self.links.send(self.key("s", "near", d), self.at(d, self.other), there, self.where(1, self.opposite))

    def joined(self, d):
        here = self.far1.at[self.index, d]
        self.links.arrived(self.key("s", "far", d), here)
        self.store(d, self.near, self.load(d, self.near) + f32(here[...]))
        there = self.near1.at[self.index, self.slot(self.side), d]
        self.links.send(self.key("s", "near", d), self.at(d, self.near), there, self.where(1, self.side))

    def first_sum(self, d):
        self.links.arrived(self.key("s", "near", d), self.near1.at[self.index, :, d])
        total = self.load(d, 0) + f32(self.near1[self.index, 0, d]) + f32(self.near1[self.index, 1, d])
        if d:
            self.store(d, 0, total)
            there = self.near2.at[self.index, d - 1]
            self.links.send(self.key("s", "near2"), self.at(d, 0), there, (self.axes[0], d))
        else:
            self.own_sum = total

    def result(self):
        self.links.arrived(self.key("s", "near2"), self.near2.at[self.index])
        total = self.own_sum
        for n in range(3):
            total = total + f32(self.near2[self.index, n])
        return total


class PlaneSum:
    def __init__(self, links, index, part, first, staged, second, y):
        self.links, self.index, self.part, self.y = links, index, part, y
        self.first, self.staged, self.second = first, staged, second
        step = part.shape[2] // 4
        self.a, self.b = pl.ds(2 * index * step, step), pl.ds((2 * index + 1) * step, step)

    def start(self):
        for n, d in enumerate((2, 1, 3)):
            self.links.send(
                ("p1a", self.index), self.part.at[:, (self.y + d) % 4, self.a], self.first.at[self.index, 0, n], ("y", d)
            )
            self.links.send(("p1b", self.index), self.part.at[d, :, self.b], self.first.at[self.index, 1, n], ("x", d))

    def second_step(self):
        totals = f32(self.part[:, pl.ds(self.y, 1), self.a, :][:, 0]), f32(self.part[0, :, self.b, :])
        for kind in range(2):
            total = totals[kind]
            self.links.arrived(("p1" + "ab"[kind], self.index), self.first.at[self.index, kind])
            for n in range(3):
                total = total + f32(self.first[self.index, kind, n])
            self.staged[self.index, kind] = total.astype(BF16)
            for n, d in enumerate((2, 1, 3)):
                other = d if kind == 0 else (self.y + d) % 4
                self.links.send(
                    ("p2" + "ab"[kind], self.index), self.staged.at[self.index, kind, other],
                    self.second.at[self.index, kind, n], ("xy"[kind], d),
                )

    def result(self):
        out = []
        for kind in range(2):
            total = f32(self.staged[self.index, 0, 0]) if kind == 0 else f32(self.staged[self.index, 1, self.y])
            self.links.arrived(("p2" + "ab"[kind], self.index), self.second.at[self.index, kind])
            for n in range(3):
                total = total + f32(self.second[self.index, kind, n])
            out.append(total)
        return out


def column_of(line):
    count = line.shape[1]
    shape = (count, count)
    diagonal = lax.broadcasted_iota(jnp.int32, shape, 0) == lax.broadcasted_iota(jnp.int32, shape, 1)
    return jnp.sum(jnp.where(diagonal, line, 0.0), axis=1, keepdims=True)


def attend(queries, keys, values, lengths, wait, index):
    width = queries.shape[1]
    heads = width // HD
    step = 16
    cache = keys.shape[1]
    own = lax.broadcasted_iota(jnp.int32, (heads * step, cache), 0) % step
    position = f32(lax.broadcasted_iota(jnp.int32, (heads * step, cache), 1))
    half_blocks = queries.shape[0] // step // 2
    blocks = range(index * half_blocks, (index + 1) * half_blocks)
    if index:
        wait("k", index)
    every = []
    for n in blocks:
        rows = slice(n * step, (n + 1) * step)
        query = queries[rows, :]
        query = jnp.concatenate([query[:, h * HD:(h + 1) * HD] for h in range(heads)], axis=0)
        every.append(lax.dot_general(
            query, keys[rows].reshape(step * cache, HD), (((1,), (1,)), ((), ())), preferred_element_type=F32
        ))
    spread = []
    for n, products in zip(blocks, every):
        scores = products[:, 0:cache]
        for r in range(1, step):
            scores = jnp.where(own == r, products[:, r * cache:(r + 1) * cache], scores)
        scores = scores * HD ** (-0.5)
        length = jnp.concatenate([lengths[n * step:(n + 1) * step]] * heads, axis=0)
        scores = jnp.where(position < length, scores, -1e30)
        exp_scores = jnp.exp(scores - jnp.max(scores, axis=1, keepdims=True))
        weights = exp_scores / jnp.sum(exp_scores, axis=1, keepdims=True)
        spread.append(jnp.concatenate([jnp.where(own == r, weights, 0.0).astype(BF16) for r in range(step)], axis=1))
    wait("v", index)
    out = []
    for n, weights in zip(blocks, spread):
        rows = slice(n * step, (n + 1) * step)
        combined = jnp.dot(weights, values[rows].reshape(step * cache, HD), preferred_element_type=F32).astype(BF16)
        out.append(jnp.concatenate([combined[h * step:(h + 1) * step] for h in range(heads)], axis=1))
    return jnp.concatenate(out, axis=0)


def kernel(
    queries, keys_hbm, values_hbm, lengths, wo_hbm, res_hbm, gain, expert_ids, gate_weights, wg_hbm, wu_hbm, wd_hbm, out,
    keys, values, wo, wg, wu, wd, res,
    part1, first1, second1, staged1,
    part2, far1, near1, near2,
    held, to_send, landed, back, returned, rows_f32, acc_gate, acc_up, squares, act,
    load_sem, send_sem, recv_sem,
):
    group = lax.axis_index("dp")
    tensor = lax.axis_index("tensor")
    x, y = tensor // 4, tensor % 4
    row_count, share = out.shape
    wide = 4 * share

    def at(i, j):
        return ((x + i) % 4) * 4 + (y + j) % 4

    to = {}
    for d in (1, 2, 3):
        to["x", d] = (group, at(d, 0))
        to["y", d] = (group, at(0, d))
    z, core = group // 2, group % 2
    for k in range(1, 8):
        to[k] = (((z + k // 2) % 4) * 2 + (core + k) % 2, tensor)
    barrier = pltpu.get_barrier_semaphore()
    for where in to:
        pl.semaphore_signal(barrier, inc=1, device_id=to[where], device_id_type=pl.DeviceIdType.MESH)
    peers = len(to)
    for name in ("x", "y"):
        to[name + "+"], to[name + "-"] = to[name, 1], to[name, 3]
    links = Links(send_sem, recv_sem, to)

    loads = {}

    def load(key, src, dst):
        pltpu.make_async_copy(src, dst, load_sem.at[loads.setdefault(key, len(loads))]).start()

    def wait(key, whole):
        pltpu.make_async_copy(whole, whole, load_sem.at[loads[key]]).wait()

    def columns(i):
        return pl.ds(pl.multiple_of(((x + i) % 4) * wide, 128), wide)

    def block_rows(i, j):
        return pl.ds(pl.multiple_of(i * wide + ((y + j) % 4) * share, 128), share)

    def block(j):
        return pl.ds(pl.multiple_of(((y + j) % 4) * share, 128), share)

    def cached(name, index):
        array = keys if name == "k" else values
        return array.at[pl.ds(index * half, half)]

    def load_cache(index):
        for name, array in (("k", keys_hbm), ("v", values_hbm)):
            load((name, index), array.at[pl.ds(index * half, half), 0], cached(name, index))

    def wait_cache(name, index):
        wait((name, index), cached(name, index))

    half = row_count // 2
    load_cache(0)
    wait_cache("k", 0)
    for i in range(4):
        load("wo", wo_hbm.at[:, columns(i)], wo.at[i])
    load_cache(1)
    load("res", res_hbm.at[:, pl.ds(pl.multiple_of(tensor * share, 128), share)], res)

    length_column = column_of(f32(lengths[...]))
    halves = [PlaneSum(links, index, part1, first1, staged1, second1, y) for index in range(2)]

    def project(attended, index):
        for i in (2, 1, 3, 0):
            product = jnp.dot(attended, wo[i], preferred_element_type=F32).astype(BF16)
            for j in range(4):
                part1[i, j, index * half:(index + 1) * half, :] = product[:, j * share:(j + 1) * share]

    attended = attend(queries, keys, values, length_column, wait_cache, 0)
    wait("wo", wo)
    project(attended, 0)
    pl.semaphore_wait(barrier, peers)
    halves[0].start()
    project(attend(queries, keys, values, length_column, wait_cache, 1), 1)
    halves[1].start()

    for i in (0, 3, 1, 2):
        load("wg", wg_hbm.at[0, columns(i)], wg.at[pl.ds(i * wide, wide)])
        load("wu", wu_hbm.at[0, columns(i)], wu.at[pl.ds(i * wide, wide)])
    for i in (2, 1, 3, 0):
        load("wd", wd_hbm.at[0, :, columns(i)], wd.at[i])

    def slot_tables():
        slots = 8 * PAD
        ids = expert_ids[...]
        relative = f32((ids // 2 - z + 4) % 4 * 2 + (ids + core) % 2)
        column = lax.broadcasted_iota(jnp.int32, (row_count, slots), 1)
        expert = f32(column // PAD)
        first = jnp.where(column_of(relative[0:1]) == expert, 1.0, 0.0)
        second = jnp.where(column_of(relative[1:2]) == expert, 1.0, 0.0)
        named = first + second
        earlier = jnp.where(
            lax.broadcasted_iota(jnp.int32, (row_count, row_count), 1)
            < lax.broadcasted_iota(jnp.int32, (row_count, row_count), 0),
            1.0,
            0.0,
        )
        rank = jnp.dot(earlier.astype(BF16), named.astype(BF16), preferred_element_type=F32)
        place = jnp.where(rank == f32(column % PAD), 1.0, 0.0)
        acc_gate[...] = jnp.zeros_like(acc_gate)
        acc_up[...] = jnp.zeros_like(acc_up)
        squares[...] = jnp.zeros_like(squares)
        return [(rows * place).astype(BF16) for rows in (first, second, named)]

    first, second, chosen = slot_tables()
    first_weight, second_weight = column_of(gate_weights[0:1]), column_of(gate_weights[1:2])
    for each in halves:
        each.second_step()
    summed = jnp.concatenate(halves[0].result() + halves[1].result(), axis=0)
    wait("res", res)
    hidden = summed + f32(res[...])
    picked = lax.dot_general(
        chosen, hidden.astype(BF16), (((0,), (0,)), ((), ())), preferred_element_type=F32
    )
    to_send[...] = picked.astype(BF16).reshape(8, PAD, share)

    for k in (1, 4, 5, 2, 3, 6, 7):
        links.send("d" if k > 1 else "d1", to_send.at[k], landed.at[k - 1], k)
    quarter = 2 * CAP
    gathers = [
        Gather(held, links, index, quarter, axes, side)
        for index, (axes, side) in enumerate((("xy", "+"), ("yx", "+"), ("yx", "-"), ("xy", "-")))
    ]

    rows_f32[0:CAP, :] = f32(to_send[0])[:CAP]
    links.arrived("d1", landed.at[0])
    rows_f32[CAP:2 * CAP, :] = f32(landed[0])[:CAP]
    held[0, 0, 0:quarter, :] = rows_f32[0:quarter, :].astype(BF16)
    gathers[0].own()
    links.arrived("d", landed.at[pl.ds(1, 6)])
    for k in range(2, 8):
        rows_f32[k * CAP:(k + 1) * CAP, :] = f32(landed[k - 1])[:CAP]
    held[0, 0, quarter:4 * quarter, :] = rows_f32[quarter:4 * quarter, :].astype(BF16)

    def consume(i, j):
        values_f32 = f32(held[i, j])
        square = values_f32 * values_f32
        folded = square[:, 0:128]
        for c in range(1, share // 128):
            folded = folded + square[:, c * 128:(c + 1) * 128]
        squares[...] += folded
        scaled = (values_f32 * f32(gain[0:1, pl.ds(pl.multiple_of(at(i, j) * share, 128), share)])).astype(BF16)
        acc_gate[...] += jnp.dot(scaled, wg[block_rows(i, j), :], preferred_element_type=F32)
        acc_up[...] += jnp.dot(scaled, wu[block_rows(i, j), :], preferred_element_type=F32)

    for each in gathers[1:]:
        each.own()
    wait("wg", wg)
    wait("wu", wu)
    consume(0, 0)
    for each in gathers:
        each.near()
    for each in gathers:
        each.pass_on(0)
    for each in gathers:
        each.far()
    for i, j in ((3, 0), (0, 3), (1, 0), (0, 1)):
        consume(i, j)
    for d in (3, 1):
        for each in gathers:
            each.pass_on(d)
    for i, j in ((3, 3), (1, 3), (3, 1), (1, 1)):
        consume(i, j)
    for each in gathers:
        each.pass_on(2)
    for d in (0, 3, 1):
        links.arrived(("g", "last", d), held.at[d, 2])
        consume(d, 2)
        consume(2, d)
    links.arrived(("g", "last", 2), held.at[2, 2])
    consume(2, 2)

    mean = jnp.sum(squares[...], axis=1, keepdims=True) * (1.0 / (16 * share))
    inverse = lax.rsqrt(mean + EPSILON)
    gate = acc_gate[...] * inverse
    up = acc_up[...] * inverse
    act[...] = (gate / (1.0 + jnp.exp(-gate)) * up).astype(BF16)
    wait("wd", wd)

    def down(i, j):
        part2[i, j] = jnp.dot(act[...], wd[i, :, block(j)], preferred_element_type=F32).astype(BF16)

    sums = [
        Sum(part2, far1, near1, near2, links, index, quarter, axes, side)
        for index, (axes, side) in enumerate((("yx", "-"), ("yx", "+"), ("xy", "+"), ("xy", "-")))
    ]
    for i, j in ORDER:
        down(i, j)
        for each in sums:
            d, along = each.place(i, j)
            if along == 2:
                each.forward(d)
    for d in (2, 1, 3, 0):
        for each in sums:
            each.joined(d)
            each.direct(d)
    for d in (2, 3, 1, 0):
        for each in sums:
            each.first_sum(d)

    empty = jnp.zeros((PAD - CAP, share), F32)

    def give_back(each):
        total = each.result()
        for k in (2 * each.index, 2 * each.index + 1):
            first_row = (k % 2) * CAP
            slot = jnp.concatenate([total[first_row:first_row + CAP], empty], axis=0).astype(BF16)
            if k == 0:
                returned[0] = slot
            else:
                back[k] = slot
                links.send("b", back.at[k], returned.at[k], (4 - k // 2) % 4 * 2 + k % 2)

    for index in (2, 3, 1, 0):
        give_back(sums[index])
    links.finish(wg)
    links.arrived("b", returned.at[pl.ds(1, 7)])
    results = returned[...].reshape(8 * PAD, share)
    layer_out = (
        hidden
        + first_weight * jnp.dot(first, results, preferred_element_type=F32)
        + second_weight * jnp.dot(second, results, preferred_element_type=F32)
    )
    out[...] = layer_out.astype(out.dtype)


def local(
    queries, key_cache, value_cache, lengths, out_proj, residual, norm_gain, expert_ids, gate_weights,
    w_gate, w_up, w_down,
):
    rows, share = queries.shape
    cache = key_cache.shape[2]
    hidden_units = w_gate.shape[2]
    slots = 8 * CAP
    vmem = pl.BlockSpec(memory_space=pltpu.VMEM)
    hbm = pl.BlockSpec(memory_space=pl.ANY)
    quarter = slots // 4
    step = rows // 4

    return pl.pallas_call(
        kernel,
        out_shape=jax.ShapeDtypeStruct((rows, share), BF16),
        in_specs=[vmem, hbm, hbm, vmem, hbm, hbm, vmem, vmem, vmem, hbm, hbm, hbm],
        out_specs=vmem,
        scratch_shapes=[
            pltpu.VMEM((rows, cache, HD), BF16),
            pltpu.VMEM((rows, cache, HD), BF16),
            pltpu.VMEM((4, share, 4 * share), BF16),
            pltpu.VMEM((16 * share, hidden_units), BF16),
            pltpu.VMEM((16 * share, hidden_units), BF16),
            pltpu.VMEM((4, hidden_units, 4 * share), BF16),
            pltpu.VMEM((rows, share), BF16),
            pltpu.VMEM((4, 4, rows, share), BF16),
            pltpu.VMEM((2, 2, 3, 4, step, share), BF16),
            pltpu.VMEM((2, 2, 3, step, share), BF16),
            pltpu.VMEM((2, 2, 4, step, share), BF16),
            pltpu.VMEM((4, 4, slots, share), BF16),
            pltpu.VMEM((4, 4, quarter, share), BF16),
            pltpu.VMEM((4, 2, 4, quarter, share), BF16),
            pltpu.VMEM((4, 3, quarter, share), BF16),
            pltpu.VMEM((4, 4, slots, share), BF16),
            pltpu.VMEM((8, PAD, share), BF16),
            pltpu.VMEM((7, PAD, share), BF16),
            pltpu.VMEM((8, PAD, share), BF16),
            pltpu.VMEM((8, PAD, share), BF16),
            pltpu.VMEM((slots, share), F32),
            pltpu.VMEM((slots, hidden_units), F32),
            pltpu.VMEM((slots, hidden_units), F32),
            pltpu.VMEM((slots, 128), F32),
            pltpu.VMEM((slots, hidden_units), BF16),
            pltpu.SemaphoreType.DMA((10,)),
            pltpu.SemaphoreType.DMA((1,)),
            pltpu.SemaphoreType.DMA((N_SEMS,)),
        ],
        compiler_params=pltpu.CompilerParams(
            collective_id=0, has_side_effects=True, vmem_limit_bytes=56 * 1024 * 1024
        ),
    )(
        queries, key_cache, value_cache, lengths.reshape(1, rows), out_proj, residual, norm_gain.reshape(1, 16 * share),
        expert_ids.T, gate_weights.T, w_gate, w_up, w_down,
    )


def solution(mesh):
    placed = (
        P("dp", "tensor"),
        P("dp", "tensor", None, None),
        P("dp", "tensor", None, None),
        P("dp"),
        P("tensor", None),
        P("dp", None),
        P(),
        P("dp", None),
        P("dp", None),
        P("dp", None, "tensor"),
        P("dp", None, "tensor"),
        P("dp", "tensor", None),
    )
    return jax.shard_map(
        local, mesh=mesh, in_specs=placed, out_specs=P("dp", "tensor"), check_vma=False
    )
```
